32 devices in a mesh: elem: 8 (over z, y), orb: 4 (over x, core).
Axes of the slice: x: 2, y: 2, z: 4, core: 2. Of those that a mesh axis runs over, the one named last changes fastest.
Arguments:
- hamiltonian: bfloat16 [256, 7, 128, 128], P('elem'), may hold values from -1 to 1, as said below
- start: bfloat16 [256, 128, 1024], P('elem', None, 'orb'), may hold values from -6 to 6
- ritz: bfloat16 [1024, 1024], P(None, 'orb'), may hold values from -0.1875 to 0.1875
Outputs:
- margin: float32 [1024, 1024], P('orb', 'elem')
- rotated: float32 [256, 128, 1024], P('elem', None, 'orb')
The draws below stay inside these ranges and needn't reach their ends.
Inputs may be any that keep to these rules, and one draw needn't show every extreme that they name: hamiltonian[e, 1 + 2 k] is the transpose of hamiltonian[n(e, 1 + 2 k), 2 + 2 k], and each diagonal block hamiltonian[e, 0] is symmetric, so the operator is symmetric.
All inputs are finite; a program needn't handle non-finite values.
Results may differ from the reference program's by a relative error of at most 0.0095.
Values may be sent and summed in bfloat16 or wider, within the bound.
A program may use at most 128 MiB of HBM per device.

```python
import math
import jax
import jax.numpy as jnp

NB = 128
NORB = 1024
GY = 4
GZ = 4
DEG = 6
GX = 16
E = 256
ROWS = 32768


def draw_hamiltonian(key, part):
    key_forward = jax.random.fold_in(key, 11)
    key_self = jax.random.fold_in(key, 12)
    key_potential = jax.random.fold_in(key, 13)
    block_scale = 0.5 / math.sqrt(7.0 * NB)
    forward = jnp.clip(jax.random.normal(key_forward, (GX, GY, GZ, 3, NB, NB), jnp.float32), -4.0, 4.0)
    raw_self = jnp.clip(jax.random.normal(key_self, (GX, GY, GZ, NB, NB), jnp.float32), -4.0, 4.0)
    forward = forward * block_scale
    potential = jax.random.uniform(key_potential, (GX, GY, GZ, NB), jnp.float32, -0.3, 0.3)
    eye_table = jnp.eye(NB, dtype=jnp.float32)
    self_block = (raw_self + jnp.swapaxes(raw_self, -1, -2)) * (block_scale / math.sqrt(2.0)) + potential[..., :, None] * eye_table
    minus_x = jnp.swapaxes(jnp.roll(forward[:, :, :, 0], 1, axis=0), -1, -2)
    minus_y = jnp.swapaxes(jnp.roll(forward[:, :, :, 1], 1, axis=1), -1, -2)
    minus_z = jnp.swapaxes(jnp.roll(forward[:, :, :, 2], 1, axis=2), -1, -2)
    stacked = jnp.stack([self_block, minus_x, forward[:, :, :, 0], minus_y, forward[:, :, :, 1], minus_z, forward[:, :, :, 2]], axis=3)
    return stacked.reshape(GX * GY * GZ, 7, NB, NB).astype(jnp.bfloat16)


def steps_of(stream_key, extent, split, low, high):
    gain = 1.0
    for dim, shards_of in split:
        heights = jax.random.uniform(jax.random.fold_in(jax.random.fold_in(stream_key, 6), dim), (shards_of,), jnp.float32, low / len(split), high / len(split))
        gain = gain * jnp.repeat(jnp.exp(heights), extent[dim] // shards_of).reshape((-1,) + (1,) * (len(extent) - 1 - dim))
    return gain


def gaussian(stream_key, extent, deviation, limit, shards=(), held_as=jnp.bfloat16):
    level = steps_of(stream_key, extent, shards, -0.22, 0.18) if shards else 1.0
    array = jax.random.normal(stream_key, extent, jnp.float32) * deviation * level
    return jnp.minimum(jnp.maximum(array, -limit), limit).astype(held_as)


def setup_inputs(seed: int = 0) -> dict:
    splits = jax.random.split(jax.random.key(seed), 4)
    return {
        "hamiltonian": draw_hamiltonian(jax.random.fold_in(splits[3], 71), 0),
        "start": gaussian(splits[1], (E, NB, NORB), 1.0, 6.0, ((0, 8), (2, 4))),
        "ritz": gaussian(splits[2], (NORB, NORB), NORB ** -0.5, 0.1875, ((1, 4),)),
    }


center_shift = 0.1
half_width = 1.25


def apply_ham(hamiltonian, rounded):
    element_grid = rounded.reshape(GX, GY, GZ, NB, NORB)
    neighbours = [element_grid,
                  jnp.roll(element_grid, 1, axis=0), jnp.roll(element_grid, -1, axis=0),
                  jnp.roll(element_grid, 1, axis=1), jnp.roll(element_grid, -1, axis=1),
                  jnp.roll(element_grid, 1, axis=2), jnp.roll(element_grid, -1, axis=2)]
    accumulated = jnp.zeros((E, NB, NORB), jnp.float32)
    for direction in range(7):
        block_set = hamiltonian[:, direction].astype(jnp.float32)
        moved = neighbours[direction].reshape(E, NB, NORB).astype(jnp.float32)
        accumulated = accumulated + jnp.einsum('eij,ejo->eio', block_set, moved)
    return accumulated


def reference(hamiltonian, start, ritz):
    previous = start.astype(jnp.float32)
    current = (apply_ham(hamiltonian, start) - center_shift * previous) / half_width
    for degree in range(DEG - 1):
        rounded = current.astype(jnp.bfloat16)
        image = apply_ham(hamiltonian, rounded)
        following = (2.0 / half_width) * (image - center_shift * current) - previous
        previous = current
        current = following
    filtered = current.astype(jnp.bfloat16).reshape(ROWS, NORB)
    margin = jnp.dot(filtered.T, filtered, preferred_element_type=jnp.float32) / float(ROWS)
    rotated = jnp.dot(filtered, ritz, preferred_element_type=jnp.float32).reshape(E, NB, NORB)
    return margin, rotated
```

```python
import functools

import jax
import jax.numpy as jnp
from jax import lax
from jax.experimental import pallas as pl
from jax.experimental.pallas import tpu as pltpu
from jax.sharding import PartitionSpec as P

NB = 128
GY = 4
GZ = 4
DEG = 6


center_shift = 0.1
half_width = 1.25


def extended(cells, sides, width):
    for axis, dim in sides:
        count = lax.axis_size(axis)
        head = lax.slice_in_dim(cells, 0, width, axis=dim)
        tail = lax.slice_in_dim(cells, cells.shape[dim] - width, cells.shape[dim], axis=dim)
        cells = jnp.concatenate(
            [
                lax.ppermute(tail, axis, [(i, (i + 1) % count) for i in range(count)]),
                cells,
                lax.ppermute(head, axis, [((i + 1) % count, i) for i in range(count)]),
            ],
            axis=dim,
        )
    return cells


def apply_ham(hamiltonian, rounded):
    elem_count = hamiltonian.shape[0]
    orb_cols = rounded.shape[2]
    layers = elem_count // (GY * GZ)
    element_grid = rounded.reshape(layers, GY, GZ, NB, orb_cols)
    padded = extended(element_grid, (("elem", 0),), 1)
    neighbours = [
        element_grid,
        padded[:-2],
        padded[2:],
        jnp.roll(element_grid, 1, axis=1),
        jnp.roll(element_grid, -1, axis=1),
        jnp.roll(element_grid, 1, axis=2),
        jnp.roll(element_grid, -1, axis=2),
    ]
    accumulated = jnp.zeros((elem_count, NB, orb_cols), jnp.float32)
    for direction in range(7):
        moved = neighbours[direction].reshape(elem_count, NB, orb_cols)
        accumulated = accumulated + jnp.einsum(
            "eij,ejo->eio", hamiltonian[:, direction], moved, preferred_element_type=jnp.float32
        )
    return accumulated


PIECES = 4


def filter_kernel(
    n, layers, ham, start, out, blocks, vec, val, halo,
    local, start_s, start_r, ham_s, ham_r, halo_s, halo_r, back_s, back_r,
):
    plane = GY * GZ
    elem_local = layers * plane
    half = start.shape[2] // 2
    merged_layers = 2 * layers
    group = plane // PIECES
    me, orb = lax.axis_index("elem"), lax.axis_index("orb")
    s = lax.rem(me, 2)
    partner = me + 1 - 2 * s
    left, right = lax.rem(me + n - 2, n), lax.rem(me + 2, n)
    across = lax.rem(orb + 2, 4)
    mate = orb + 1 - 2 * lax.rem(orb, 2)
    diagonal = lax.rem(mate + 2, 4)

    barrier = pltpu.get_barrier_semaphore()
    for target in ({"elem": partner}, {"elem": left}, {"elem": right}, {"orb": across}, {"orb": mate}):
        pl.semaphore_signal(barrier, inc=1, device_id=target, device_id_type=pl.DeviceIdType.MESH)

    def lanes(part):
        return pl.ds(pl.multiple_of(part * half, half), half)

    def layer_of(side, first):
        return side * first + (1 - side) * (1 - first)

    own_h = pltpu.make_async_copy(ham, blocks.at[pl.ds(s * elem_local, elem_local)], local.at[0])
    own_v = pltpu.make_async_copy(
        start.at[:, :, lanes(s)], vec.at[0, pl.ds(s * elem_local, elem_local)], local.at[1]
    )
    own_v.start()
    own_h.start()
    pl.semaphore_wait(barrier, 5)

    def start_copy(first):
        base = layer_of(s, first) * plane
        return pltpu.make_async_remote_copy(
            src_ref=start.at[pl.ds(base, plane), :, lanes(1 - s)],
            dst_ref=vec.at[0, pl.ds(s * elem_local + base, plane)],
            send_sem=start_s.at[first], recv_sem=start_r.at[first],
            device_id={"elem": partner}, device_id_type=pl.DeviceIdType.MESH,
        )

    def place(side, c, q):
        first = 1 - c // PIECES
        return side * elem_local + layer_of(side, first) * plane + lax.rem(c, PIECES) * group + q

    def ham_y(c):
        at = place(s, c, orb)
        return pltpu.make_async_remote_copy(
            src_ref=ham.at[at - s * elem_local], dst_ref=blocks.at[at],
            send_sem=ham_s.at[0, c], recv_sem=ham_r.at[0, c],
            device_id={"elem": partner}, device_id_type=pl.DeviceIdType.MESH,
        )

    def ham_on(kind, c, q, to):
        at = place(1 - s, c, q)
        return pltpu.make_async_remote_copy(
            src_ref=blocks.at[at], dst_ref=blocks.at[at],
            send_sem=ham_s.at[kind, c], recv_sem=ham_r.at[kind, c],
            device_id={"orb": to}, device_id_type=pl.DeviceIdType.MESH,
        )

    def halo_copy(k, side, c):
        layer = 0 if side == 1 else merged_layers - 1
        return pltpu.make_async_remote_copy(
            src_ref=vec.at[lax.rem(k, 2), pl.ds(layer * plane + c * group, group)],
            dst_ref=halo.at[k, side, pl.ds(c * group, group)],
            send_sem=halo_s.at[k, side, c], recv_sem=halo_r.at[k, side, c],
            device_id={"elem": left if side == 1 else right}, device_id_type=pl.DeviceIdType.MESH,
        )

    start_copy(1).start()
    start_copy(0).start()

    @pl.loop(0, 2 * PIECES)
    def _(c):
        ham_y(c).start()

    own_v.wait()
    start_copy(1).wait_recv()

    @pl.loop(0, PIECES)
    def _(c):
        halo_copy(0, 0, c).start()
        halo_copy(0, 1, c).start()

    start_copy(0).wait_recv()

    @pl.loop(0, 2 * elem_local)
    def _(i):
        val[0, i] = vec[0, i].astype(jnp.float32)
        val[1, i] = jnp.zeros((NB, half), jnp.float32)

    own_h.wait()

    def forward(c):
        ham_y(c).wait_recv()
        ham_on(1, c, orb, across).start()
        ham_on(2, c, orb, mate).start()

    def finish(c):
        ham_on(1, c, across, across).wait_recv()
        ham_on(3, c, across, mate).start()
        ham_on(2, c, mate, mate).wait_recv()
        ham_on(3, c, diagonal, mate).wait_recv()

    def bring(first, last):
        forward(first)

        @pl.loop(first, last - 1)
        def _(c):
            forward(c + 1)
            finish(c)

        finish(last - 1)

    def element(k, at, below, above):
        now, later = lax.rem(k, 2), lax.rem(k + 1, 2)
        j = lax.rem(at, plane)
        base = at - j
        jy, jz = j // GZ, lax.rem(j, GZ)
        around = [
            lax.rem(jy + GY - 1, GY) * GZ + jz,
            lax.rem(jy + 1, GY) * GZ + jz,
            jy * GZ + lax.rem(jz + GZ - 1, GZ),
            jy * GZ + lax.rem(jz + 1, GZ),
        ]
        rhs = jnp.concatenate(
            [vec[now, at], below, above] + [vec[now, base + other] for other in around], axis=0
        )
        lhs = jnp.concatenate([blocks[at, d] for d in range(7)], axis=1)
        image = jnp.dot(lhs, rhs, preferred_element_type=jnp.float32)
        first = k == 0
        scale = jnp.where(first, 1.0 / half_width, 2.0 / half_width)
        keep = jnp.where(first, 0.0, 1.0)
        value = scale * (image - center_shift * val[now, at]) - keep * val[later, at]
        val[later, at] = value
        vec[later, at] = value.astype(jnp.bfloat16)

    def edges(k, send):
        now = lax.rem(k, 2)

        @pl.loop(0, PIECES)
        def _(c):
            for side, layer in ((0, 0), (1, merged_layers - 1)):
                halo_copy(k, side, c).wait_recv()

                @pl.when(k >= 1)
                def _():
                    halo_copy(k - 1, 1 - side, c).wait_send()

                for i in range(group):
                    j = c * group + i
                    at = layer * plane + j
                    if side == 0:
                        element(k, at, halo[k, 0, j], vec[now, at + plane])
                    else:
                        element(k, at, vec[now, at - plane], halo[k, 1, j])
                if send:
                    halo_copy(k + 1, 1 - side, c).start()

    def interior(k):
        now = lax.rem(k, 2)

        @pl.loop(plane // group, (merged_layers - 1) * plane // group)
        def _(c):
            for i in range(group):
                at = c * group + i
                element(k, at, vec[now, at - plane], vec[now, at + plane])

    bring(0, PIECES)

    @pl.loop(0, DEG - 1)
    def _(k):
        edges(k, True)

        @pl.when(k == 0)
        def _():
            bring(PIECES, 2 * PIECES)

        interior(k)

    last = DEG % 2

    def back_copy(first):
        base = layer_of(1 - s, first) * plane
        return pltpu.make_async_remote_copy(
            src_ref=vec.at[last, pl.ds((1 - s) * elem_local + base, plane)],
            dst_ref=out.at[pl.ds(base, plane), :, lanes(s)],
            send_sem=back_s.at[first], recv_sem=back_r.at[first],
            device_id={"elem": partner}, device_id_type=pl.DeviceIdType.MESH,
        )

    def back_wait(first):
        base = layer_of(s, first) * plane
        return pltpu.make_async_remote_copy(
            src_ref=vec.at[last, pl.ds(s * elem_local + base, plane)],
            dst_ref=out.at[pl.ds(base, plane), :, lanes(1 - s)],
            send_sem=back_s.at[first], recv_sem=back_r.at[first],
            device_id={"elem": partner}, device_id_type=pl.DeviceIdType.MESH,
        )

    interior(DEG - 1)
    back_copy(0).start()
    edges(DEG - 1, False)
    back_copy(1).start()
    keep_own = pltpu.make_async_copy(
        vec.at[last, pl.ds(s * elem_local, elem_local)], out.at[:, :, lanes(s)], local.at[1]
    )
    keep_own.start()

    @pl.loop(0, 2 * PIECES)
    def _(c):
        ham_y(c).wait_send()
        ham_on(1, c, orb, across).wait_send()
        ham_on(2, c, orb, mate).wait_send()
        ham_on(3, c, across, mate).wait_send()

    @pl.loop(0, PIECES)
    def _(c):
        halo_copy(DEG - 1, 0, c).wait_send()
        halo_copy(DEG - 1, 1, c).wait_send()

    for first in (0, 1):
        start_copy(first).wait_send()
        back_copy(first).wait_send()
        back_wait(first).wait_recv()
    keep_own.wait()


def merged_filter(hamiltonian, start):
    n = lax.axis_size("elem")
    elem_local, _, orb_cols = start.shape
    layers = elem_local // (GY * GZ)
    half = orb_cols // 2
    dma = pltpu.SemaphoreType.DMA
    return pl.pallas_call(
        functools.partial(filter_kernel, n, layers),
        out_shape=jax.ShapeDtypeStruct(start.shape, jnp.bfloat16),
        in_specs=[pl.BlockSpec(memory_space=pl.ANY)] * 2,
        out_specs=pl.BlockSpec(memory_space=pl.ANY),
        scratch_shapes=[
            pltpu.VMEM((2 * elem_local, 7, NB, NB), jnp.bfloat16),
            pltpu.VMEM((2, 2 * elem_local, NB, half), jnp.bfloat16),
            pltpu.VMEM((2, 2 * elem_local, NB, half), jnp.float32),
            pltpu.VMEM((DEG, 2, GY * GZ, NB, half), jnp.bfloat16),
            dma((2,)),
            dma((2,)), dma((2,)),
            dma((4, 2 * PIECES)), dma((4, 2 * PIECES)),
            dma((DEG, 2, PIECES)), dma((DEG, 2, PIECES)),
            dma((2,)), dma((2,)),
        ],
        compiler_params=pltpu.CompilerParams(
            collective_id=0, has_side_effects=True, vmem_limit_bytes=48 * 1024 * 1024
        ),
        cost_estimate=pl.CostEstimate(
            flops=2 * DEG * 7 * elem_local * NB * NB * orb_cols,
            bytes_accessed=hamiltonian.size * 2 + start.size * 4, transcendentals=0,
        ),
    )(hamiltonian, start)


def plain_filter(hamiltonian, start):
    previous = start.astype(jnp.float32)
    current = (apply_ham(hamiltonian, start) - center_shift * previous) / half_width
    for degree in range(DEG - 1):
        rounded = current.astype(jnp.bfloat16)
        image = apply_ham(hamiltonian, rounded)
        following = 2.0 / half_width * (image - center_shift * current) - previous
        previous = current
        current = following
    return current.astype(jnp.bfloat16)


def on_device(hamiltonian, start, ritz):
    elem_count = hamiltonian.shape[0]
    orb_cols = start.shape[2]
    local_rows = elem_count * NB
    rows_total = float(local_rows * lax.axis_size("elem"))
    slabs = lax.axis_size("elem")
    can_merge = (
        slabs % 2 == 0 and slabs >= 6 and lax.axis_size("orb") == 4
        and orb_cols % 256 == 0 and elem_count == 2 * GY * GZ
    )
    filtered = (merged_filter if can_merge else plain_filter)(hamiltonian, start)
    filtered = filtered.reshape(local_rows, orb_cols)
    panel_cols = lax.all_gather(filtered, "orb", axis=1, tiled=True)
    block_part = jnp.einsum("ri,rj->ij", filtered, panel_cols, preferred_element_type=jnp.float32)
    margin_rows = block_part
    rotated_part = jnp.dot(panel_cols, ritz, preferred_element_type=jnp.float32)
    margin_rows, rotated_local = (margin_rows, rotated_part)
    margin_block = (
        lax.psum_scatter(
            margin_rows.astype(jnp.bfloat16), "elem", scatter_dimension=1, tiled=True
        ).astype(jnp.float32)
        / rows_total
    )
    return (margin_block, rotated_local.reshape(elem_count, NB, orb_cols))


def solution(mesh):
    in_specs = (P("elem", None, None, None), P("elem", None, "orb"), P(None, "orb"))
    out_specs = (P("orb", "elem"), P("elem", None, "orb"))
    return jax.shard_map(
        on_device, mesh=mesh, in_specs=in_specs, out_specs=out_specs, check_vma=False
    )
```

```python
import functools

import jax
import jax.numpy as jnp
from jax import lax
from jax.experimental import pallas as pl
from jax.experimental.pallas import tpu as pltpu
from jax.sharding import PartitionSpec as P

NB = 128
GY = 4
GZ = 4
DEG = 6


center_shift = 0.1
half_width = 1.25


def extended(cells, sides, width):
    for axis, dim in sides:
        count = lax.axis_size(axis)
        head = lax.slice_in_dim(cells, 0, width, axis=dim)
        tail = lax.slice_in_dim(cells, cells.shape[dim] - width, cells.shape[dim], axis=dim)
        cells = jnp.concatenate(
            [
                lax.ppermute(tail, axis, [(i, (i + 1) % count) for i in range(count)]),
                cells,
                lax.ppermute(head, axis, [((i + 1) % count, i) for i in range(count)]),
            ],
            axis=dim,
        )
    return cells


def apply_ham(hamiltonian, rounded):
    elem_count = hamiltonian.shape[0]
    orb_cols = rounded.shape[2]
    layers = elem_count // (GY * GZ)
    element_grid = rounded.reshape(layers, GY, GZ, NB, orb_cols)
    padded = extended(element_grid, (("elem", 0),), 1)
    neighbours = [
        element_grid,
        padded[:-2],
        padded[2:],
        jnp.roll(element_grid, 1, axis=1),
        jnp.roll(element_grid, -1, axis=1),
        jnp.roll(element_grid, 1, axis=2),
        jnp.roll(element_grid, -1, axis=2),
    ]
    accumulated = jnp.zeros((elem_count, NB, orb_cols), jnp.float32)
    for direction in range(7):
        moved = neighbours[direction].reshape(elem_count, NB, orb_cols)
        accumulated = accumulated + jnp.einsum(
            "eij,ejo->eio", hamiltonian[:, direction], moved, preferred_element_type=jnp.float32
        )
    return accumulated


PIECES = 4


def filter_kernel(
    n, layers, ham, start, ritz, margin, rotated, blocks, vec, val, halo, panel, turn, product, total, parts, came,
    local, start_s, start_r, ham_s, ham_r, halo_s, halo_r, gather_s, gather_r, part_s, part_r, out_s,
):
    plane = GY * GZ
    elem_local = layers * plane
    half = start.shape[2] // 2
    merged_layers = 2 * layers
    group = plane // PIECES
    me, orb = lax.axis_index("elem"), lax.axis_index("orb")
    s = lax.rem(me, 2)
    partner = me + 1 - 2 * s
    left, right = lax.rem(me + n - 2, n), lax.rem(me + 2, n)
    across = lax.rem(orb + 2, 4)
    mate = orb + 1 - 2 * lax.rem(orb, 2)
    diagonal = lax.rem(mate + 2, 4)

    barrier = pltpu.get_barrier_semaphore()
    peers = [{"elem": lax.rem(me + d, n)} for d in range(1, n)]
    for target in peers + [{"orb": across}, {"orb": mate}]:
        pl.semaphore_signal(barrier, inc=1, device_id=target, device_id_type=pl.DeviceIdType.MESH)

    def lanes(part):
        return pl.ds(pl.multiple_of(part * half, half), half)

    def layer_of(side, first):
        return side * first + (1 - side) * (1 - first)

    own_h = pltpu.make_async_copy(ham, blocks.at[pl.ds(s * elem_local, elem_local)], local.at[0])
    own_v = pltpu.make_async_copy(
        start.at[:, :, lanes(s)], vec.at[0, pl.ds(s * elem_local, elem_local)], local.at[1]
    )
    own_v.start()
    own_h.start()
    own_r = pltpu.make_async_copy(ritz, turn, local.at[2])
    own_r.start()
    pl.semaphore_wait(barrier, n + 1)

    def start_copy(first):
        base = layer_of(s, first) * plane
        return pltpu.make_async_remote_copy(
            src_ref=start.at[pl.ds(base, plane), :, lanes(1 - s)],
            dst_ref=vec.at[0, pl.ds(s * elem_local + base, plane)],
            send_sem=start_s.at[first], recv_sem=start_r.at[first],
            device_id={"elem": partner}, device_id_type=pl.DeviceIdType.MESH,
        )

    def place(side, c, q):
        first = 1 - c // PIECES
        return side * elem_local + layer_of(side, first) * plane + lax.rem(c, PIECES) * group + q

    def ham_y(c):
        at = place(s, c, orb)
        return pltpu.make_async_remote_copy(
            src_ref=ham.at[at - s * elem_local], dst_ref=blocks.at[at],
            send_sem=ham_s.at[0, c], recv_sem=ham_r.at[0, c],
            device_id={"elem": partner}, device_id_type=pl.DeviceIdType.MESH,
        )

    def ham_on(kind, c, q, to):
        at = place(1 - s, c, q)
        return pltpu.make_async_remote_copy(
            src_ref=blocks.at[at], dst_ref=blocks.at[at],
            send_sem=ham_s.at[kind, c], recv_sem=ham_r.at[kind, c],
            device_id={"orb": to}, device_id_type=pl.DeviceIdType.MESH,
        )

    def halo_copy(k, side, c):
        layer = 0 if side == 1 else merged_layers - 1
        return pltpu.make_async_remote_copy(
            src_ref=vec.at[lax.rem(k, 2), pl.ds(layer * plane + c * group, group)],
            dst_ref=halo.at[k, side, pl.ds(c * group, group)],
            send_sem=halo_s.at[k, side, c], recv_sem=halo_r.at[k, side, c],
            device_id={"elem": left if side == 1 else right}, device_id_type=pl.DeviceIdType.MESH,
        )

    start_copy(1).start()
    start_copy(0).start()

    @pl.loop(0, 2 * PIECES)
    def _(c):
        ham_y(c).start()

    own_v.wait()
    start_copy(1).wait_recv()

    @pl.loop(0, PIECES)
    def _(c):
        halo_copy(0, 0, c).start()
        halo_copy(0, 1, c).start()

    start_copy(0).wait_recv()

    @pl.loop(0, 2 * elem_local)
    def _(i):
        val[0, i] = vec[0, i].astype(jnp.float32)
        val[1, i] = jnp.zeros((NB, half), jnp.float32)

    own_h.wait()

    def forward(c):
        ham_y(c).wait_recv()
        ham_on(1, c, orb, across).start()
        ham_on(2, c, orb, mate).start()

    def finish(c):
        ham_on(1, c, across, across).wait_recv()
        ham_on(3, c, across, mate).start()
        ham_on(2, c, mate, mate).wait_recv()
        ham_on(3, c, diagonal, mate).wait_recv()

    def bring(first, last):
        forward(first)

        @pl.loop(first, last - 1)
        def _(c):
            forward(c + 1)
            finish(c)

        finish(last - 1)

    def element(k, at, below, above):
        now, later = lax.rem(k, 2), lax.rem(k + 1, 2)
        j = lax.rem(at, plane)
        base = at - j
        jy, jz = j // GZ, lax.rem(j, GZ)
        around = [
            lax.rem(jy + GY - 1, GY) * GZ + jz,
            lax.rem(jy + 1, GY) * GZ + jz,
            jy * GZ + lax.rem(jz + GZ - 1, GZ),
            jy * GZ + lax.rem(jz + 1, GZ),
        ]
        rhs = jnp.concatenate(
            [vec[now, at], below, above] + [vec[now, base + other] for other in around], axis=0
        )
        lhs = jnp.concatenate([blocks[at, d] for d in range(7)], axis=1)
        image = jnp.dot(lhs, rhs, preferred_element_type=jnp.float32)
        first = k == 0
        scale = jnp.where(first, 1.0 / half_width, 2.0 / half_width)
        keep = jnp.where(first, 0.0, 1.0)
        value = scale * (image - center_shift * val[now, at]) - keep * val[later, at]
        val[later, at] = value
        vec[later, at] = value.astype(jnp.bfloat16)

    def edges(k, after):
        now = lax.rem(k, 2)

        @pl.loop(0, PIECES)
        def _(c):
            for side, layer in ((0, 0), (1, merged_layers - 1)):
                halo_copy(k, side, c).wait_recv()

                @pl.when(k >= 1)
                def _():
                    halo_copy(k - 1, 1 - side, c).wait_send()

                for i in range(group):
                    j = c * group + i
                    at = layer * plane + j
                    if side == 0:
                        element(k, at, halo[k, 0, j], vec[now, at + plane])
                    else:
                        element(k, at, vec[now, at - plane], halo[k, 1, j])
                if after is None:
                    halo_copy(k + 1, 1 - side, c).start()
            if after is not None:
                after(c)

    def interior(k):
        now = lax.rem(k, 2)

        @pl.loop(plane // group, (merged_layers - 1) * plane // group)
        def _(c):
            for i in range(group):
                at = c * group + i
                element(k, at, vec[now, at - plane], vec[now, at + plane])

    bring(0, PIECES)

    @pl.loop(0, DEG - 1)
    def _(k):
        edges(k, None)

        @pl.when(k == 0)
        def _():
            bring(PIECES, 2 * PIECES)

        interior(k)

    last = DEG % 2

    def rows(side, c):
        return layer_of(side, c // PIECES) * plane + lax.rem(c, PIECES) * group

    def to_partner(c):
        at = rows(1 - s, c)
        return pltpu.make_async_remote_copy(
            src_ref=vec.at[last, pl.ds((1 - s) * elem_local + at, group)],
            dst_ref=panel.at[2 * orb + s, pl.ds(at, group)],
            send_sem=gather_s.at[0, c], recv_sem=gather_r.at[0, c],
            device_id={"elem": partner}, device_id_type=pl.DeviceIdType.MESH,
        )

    def to_orb(kind, h, c):
        block = 2 * (across if kind == 2 else orb) + (s if h == 0 else 1 - s)
        at = panel.at[block, pl.ds(rows(s, c), group)]
        return pltpu.make_async_remote_copy(
            src_ref=at, dst_ref=at,
            send_sem=gather_s.at[1 + 2 * kind + h, c], recv_sem=gather_r.at[1 + 2 * kind + h, c],
            device_id={"orb": across if kind == 0 else mate}, device_id_type=pl.DeviceIdType.MESH,
        )

    def offer(c):
        to_partner(c).start()
        at = rows(s, c)
        panel[2 * orb + s, pl.ds(at, group)] = vec[last, pl.ds(s * elem_local + at, group)]
        to_orb(0, 0, c).start()
        to_orb(1, 0, c).start()

    def pass_on(c):
        to_partner(c).wait_recv()
        to_orb(0, 1, c).start()
        to_orb(1, 1, c).start()

    def relay(c):
        for h in (0, 1):
            to_orb(0, h, c).wait_recv()
            to_orb(2, h, c).start()

    def complete(c):
        for kind in (1, 2):
            for h in (0, 1):
                to_orb(kind, h, c).wait_recv()

    def result_copy(c):
        at = pl.ds(rows(s, c), group)
        return pltpu.make_async_copy(product.at[at], rotated.at[at], out_s.at[c])

    def multiply(c):
        at = pl.ds(rows(s, c), group)
        whole = jnp.concatenate([panel[b, at].reshape(group * NB, half) for b in range(n)], axis=1)
        mine = jnp.concatenate(
            [panel[2 * orb + h, at].reshape(group * NB, half) for h in (0, 1)], axis=1
        )
        result = jnp.dot(whole, turn[...], preferred_element_type=jnp.float32)
        product[at] = result.reshape(group, NB, 2 * half)
        result_copy(c).start()
        total[...] += lax.dot_general(
            mine, whole, (((0,), (0,)), ((), ())), preferred_element_type=jnp.float32
        )

    interior(DEG - 1)

    @pl.loop(0, PIECES)
    def _(c):
        offer(c)

    total[...] = jnp.zeros_like(total)

    def after(c):
        offer(PIECES + c)
        pass_on(c)

    edges(DEG - 1, after)
    own_r.wait()
    relay(0)

    @pl.loop(0, PIECES)
    def _(c):
        pass_on(PIECES + c)
        relay(c + 1)
        complete(c)
        multiply(c)

    @pl.loop(PIECES, 2 * PIECES)
    def _(c):
        @pl.when(c + 1 < 2 * PIECES)
        def _():
            relay(c + 1)

        complete(c)
        multiply(c)

    def part_copy(d):
        to = lax.rem(me + d, n)
        return pltpu.make_async_remote_copy(
            src_ref=parts.at[to], dst_ref=came.at[d - 1],
            send_sem=part_s.at[d - 1], recv_sem=part_r.at[d - 1],
            device_id={"elem": to}, device_id_type=pl.DeviceIdType.MESH,
        )

    for i in range(n):
        parts[i] = total[:, i * half : (i + 1) * half].astype(jnp.bfloat16)
    for d in range(1, n):
        part_copy(d).start()

    @pl.loop(0, 2 * PIECES)
    def _(c):
        ham_y(c).wait_send()
        ham_on(1, c, orb, across).wait_send()
        ham_on(2, c, orb, mate).wait_send()
        ham_on(3, c, across, mate).wait_send()
        to_partner(c).wait_send()
        for kind in range(3):
            for h in (0, 1):
                to_orb(kind, h, c).wait_send()
        result_copy(c).wait()

    @pl.loop(0, PIECES)
    def _(c):
        halo_copy(DEG - 1, 0, c).wait_send()
        halo_copy(DEG - 1, 1, c).wait_send()

    for first in (0, 1):
        start_copy(first).wait_send()
    sums = total[:, lanes(me)]
    for d in range(1, n):
        part_copy(d).wait_recv()
        sums = sums + came[d - 1].astype(jnp.float32)
    margin[...] = sums / float(n * elem_local * NB)
    for d in range(1, n):
        part_copy(d).wait_send()


def merged(hamiltonian, start, ritz):
    n = lax.axis_size("elem")
    elem_local, _, orb_cols = start.shape
    layers = elem_local // (GY * GZ)
    half = orb_cols // 2
    dma = pltpu.SemaphoreType.DMA
    return pl.pallas_call(
        functools.partial(filter_kernel, n, layers),
        out_shape=(
            jax.ShapeDtypeStruct((orb_cols, half), jnp.float32),
            jax.ShapeDtypeStruct(start.shape, jnp.float32),
        ),
        in_specs=[pl.BlockSpec(memory_space=pl.ANY)] * 3,
        out_specs=(pl.BlockSpec(memory_space=pltpu.VMEM), pl.BlockSpec(memory_space=pl.ANY)),
        scratch_shapes=[
            pltpu.VMEM((2 * elem_local, 7, NB, NB), jnp.bfloat16),
            pltpu.VMEM((2, 2 * elem_local, NB, half), jnp.bfloat16),
            pltpu.VMEM((2, 2 * elem_local, NB, half), jnp.float32),
            pltpu.VMEM((DEG, 2, GY * GZ, NB, half), jnp.bfloat16),
            pltpu.VMEM((n, elem_local, NB, half), jnp.bfloat16),
            pltpu.VMEM(ritz.shape, jnp.bfloat16),
            pltpu.VMEM(start.shape, jnp.float32),
            pltpu.VMEM((orb_cols, n * half), jnp.float32),
            pltpu.VMEM((n, orb_cols, half), jnp.bfloat16),
            pltpu.VMEM((n - 1, orb_cols, half), jnp.bfloat16),
            dma((3,)),
            dma((2,)), dma((2,)),
            dma((4, 2 * PIECES)), dma((4, 2 * PIECES)),
            dma((DEG, 2, PIECES)), dma((DEG, 2, PIECES)),
            dma((7, 2 * PIECES)), dma((7, 2 * PIECES)),
            dma((n - 1,)), dma((n - 1,)),
            dma((2 * PIECES,)),
        ],
        compiler_params=pltpu.CompilerParams(
            collective_id=0, has_side_effects=True, vmem_limit_bytes=60 * 1024 * 1024
        ),
        cost_estimate=pl.CostEstimate(
            flops=2 * elem_local * NB * orb_cols * (DEG * 7 * NB + 2 * n * half),
            bytes_accessed=hamiltonian.size * 2 + start.size * 6, transcendentals=0,
        ),
    )(hamiltonian, start, ritz)


def plain_filter(hamiltonian, start):
    previous = start.astype(jnp.float32)
    current = (apply_ham(hamiltonian, start) - center_shift * previous) / half_width
    for degree in range(DEG - 1):
        rounded = current.astype(jnp.bfloat16)
        image = apply_ham(hamiltonian, rounded)
        following = 2.0 / half_width * (image - center_shift * current) - previous
        previous = current
        current = following
    return current.astype(jnp.bfloat16)


def on_device(hamiltonian, start, ritz):
    elem_count = hamiltonian.shape[0]
    orb_cols = start.shape[2]
    local_rows = elem_count * NB
    rows_total = float(local_rows * lax.axis_size("elem"))
    slabs = lax.axis_size("elem")
    can_merge = (
        slabs % 2 == 0 and slabs >= 6 and lax.axis_size("orb") == 4
        and orb_cols == 2 * NB and ritz.shape[0] == slabs * NB and elem_count == 2 * GY * GZ
    )
    if can_merge:
        return merged(hamiltonian, start, ritz)
    filtered = plain_filter(hamiltonian, start)
    filtered = filtered.reshape(local_rows, orb_cols)
    panel_cols = lax.all_gather(filtered, "orb", axis=1, tiled=True)
    block_part = jnp.einsum("ri,rj->ij", filtered, panel_cols, preferred_element_type=jnp.float32)
    margin_rows = block_part
    rotated_part = jnp.dot(panel_cols, ritz, preferred_element_type=jnp.float32)
    margin_rows, rotated_local = (margin_rows, rotated_part)
    margin_block = (
        lax.psum_scatter(
            margin_rows.astype(jnp.bfloat16), "elem", scatter_dimension=1, tiled=True
        ).astype(jnp.float32)
        / rows_total
    )
    return (margin_block, rotated_local.reshape(elem_count, NB, orb_cols))


def solution(mesh):
    in_specs = (P("elem", None, None, None), P("elem", None, "orb"), P(None, "orb"))
    out_specs = (P("orb", "elem"), P("elem", None, "orb"))
    return jax.shard_map(
        on_device, mesh=mesh, in_specs=in_specs, out_specs=out_specs, check_vma=False
    )
```
